32 devices in a mesh: seq: 8 (over z, x), head: 4 (over y, core).
Axes of the slice: x: 2, y: 2, z: 4, core: 2. Of those that a mesh axis runs over, the one named last changes fastest.
Arguments:
- tokens: bfloat16 [1024, 4, 2048], P('seq', None, 'head'), may hold values from -6 to 6
- attn_gain: bfloat16 [2048], replicated, may hold values from 0.25 to 1.75
- query_weight: bfloat16 [2048, 2048], P(None, 'head'), may hold values from -0.125 to 0.125
- key_weight: bfloat16 [2048, 2048], P(None, 'head'), may hold values from -0.125 to 0.125
- value_weight: bfloat16 [2048, 2048], P(None, 'head'), may hold values from -0.125 to 0.125
- head_gain: bfloat16 [2048], P('head'), may hold values from 0.25 to 1.75
- out_weight: bfloat16 [2048, 2048], P('head'), may hold values from -0.125 to 0.125
- moe_gain: bfloat16 [2048], replicated, may hold values from 0.25 to 1.75
- route_ids: int32 [1024, 4, 8], P(('seq', 'head')), may hold values from 0 to 63, all different within a row; in each aligned block of 128 rows (0 to 127, 128 to 255, ..., all dimensions but the last counted through in order) at most 24 rows name the same one
- route_weight: float32 [1024, 4, 8], P(('seq', 'head')), may hold values from 0.05 to 0.3
- expert_gate: bfloat16 [128, 2048, 512], P(('seq', 'head')), may hold values from -0.125 to 0.125
- expert_up: bfloat16 [128, 2048, 512], P(('seq', 'head')), may hold values from -0.125 to 0.125
- expert_down: bfloat16 [128, 512, 2048], P(('seq', 'head')), may hold values from -0.1875 to 0.1875
Outputs:
- layer_output: bfloat16 [1024, 4, 2048], P(('seq', 'head'))
The draws below stay inside these ranges and needn't reach their ends.
Inputs may be any that keep to these rules, and one draw needn't show every extreme that they name: `route_ids`: the rows [position, sequence] taken position-major form aligned blocks of 128 rows, the rows of one device; within every block no expert is named by more than 24 routes, and in every draw some block has an expert named by exactly 24 routes. The 8 experts of a row differ.
All inputs are finite; a program needn't handle non-finite values.
Results may differ from the reference program's by a relative error of at most 0.017.
Values may be sent and summed in bfloat16 or wider, within the bound.
A program may use at most 128 MiB of HBM per device.

```python
import math
import jax
import jax.numpy as jnp
import numpy as np
from jax import lax

D = 2048
HEADS = 16
HEAD_DIM = 128
FF = 1024
EXPERTS = 64
TOP = 8
BATCH = 4
SPAN = 128
LENGTH = 1024
ROWS = 128
CAP = 24
N_SEQ = 8
N_HEAD = 4
DEVICES = 32


def levels(stream_key, extent, cuts, least, largest):
    def one(dim, parts):
        draws = jax.random.uniform(jax.random.fold_in(jax.random.fold_in(stream_key, 6), dim), (parts,), jnp.float32, least / len(cuts), largest / len(cuts))
        return jnp.repeat(jnp.exp(draws), extent[dim] // parts).reshape((-1,) + (1,) * (len(extent) - dim - 1))

    factor_of = one(*cuts[0])
    for cut in cuts[1:]:
        factor_of = factor_of * one(*cut)
    return factor_of


def deal_out(rng, own, number, rows, count, top, most, lean):
    order = jax.random.permutation(rng, count)
    crowded, usual = load_shares(count, rows * top, most, lean, True), load_shares(count, rows * top, most, lean, False)
    places = jnp.arange(count)

    def named(tallies, turn):
        used = int((tallies > 0).sum())
        fixed = max(1, used // 4)
        moved = fixed + (places - fixed + turn * (used - fixed)) % max(1, count - fixed)
        return jnp.zeros((count,), jnp.int32).at[order[jnp.where(places < fixed, places, moved)]].set(jnp.asarray(tallies, jnp.int32))

    tallies = jnp.where(number % 4 == 0, named(crowded, number // 4), named(usual, number - number // 4 - 1))
    mixed = jax.random.permutation(jax.random.fold_in(own, 3), count)
    donor, taker = mixed[0:count // 2 * 2:2], mixed[1:count // 2 * 2:2]
    margin = jnp.minimum(tallies[donor] - 1, most - tallies[taker]) // 2
    margin = jnp.where((donor == order[0]) | (taker == order[0]) | (tallies[taker] == 0), 0, jnp.maximum(margin, 0))
    moved = jax.random.randint(jax.random.fold_in(own, 4), (count // 2,), 0, 1 << 20) % (margin + 1)
    tallies = tallies.at[donor].add(-moved).at[taker].add(moved)
    items = jnp.searchsorted(jnp.cumsum(tallies), jnp.arange(rows * top), side="right").astype(jnp.int32)
    grid = items.reshape(top, rows).T
    grid = grid[jax.random.permutation(jax.random.fold_in(own, 1), rows)]
    turn = jax.random.randint(jax.random.fold_in(own, 2), (rows, 1), 0, top)
    return jnp.take_along_axis(grid, (jnp.arange(top)[None, :] + turn) % top, axis=1)


def load_shares(amount, total, most, slope, full):
    portions = [(1 << 20) // math.isqrt(standing ** slope) + 1 for standing in range(1, amount + 1)]
    largest = most if full else min(most, max(-(-total // amount), total * portions[0] // sum(portions)))
    least = 1 if total - largest >= amount - 1 else 0
    holding, rest = [largest] + [least] * (amount - 1), total - largest - least * (amount - 1)
    while rest > 0:
        candidates = [i for i in range(1, amount) if holding[i] < largest] or [i for i in range(1, amount) if holding[i] < most]
        mass, remaining = sum([portions[i] for i in candidates]), rest
        for i in candidates:
            more = min(most - holding[i], max(1, remaining * portions[i] // mass), rest)
            holding[i] = holding[i] + more
            rest = rest - more
    return np.array(holding)


def bell_draw(key, shape, scale, reach, shards=(), kind=jnp.bfloat16):
    level = levels(key, shape, shards, -0.22, 0.18) if shards else 1.0
    values = jax.random.normal(key, shape, jnp.float32) * scale * level
    return jnp.minimum(jnp.maximum(values, -reach), reach).astype(kind)


def setup_inputs(seed: int = 0) -> dict:
    key_list = jax.random.split(jax.random.key(seed), 14)
    tokens = bell_draw(key_list[0], (LENGTH, BATCH, D), 1.0, 6.0, ((0, 8), (2, 4)))
    attn_gain = jnp.clip(1.0 + 0.15 * jax.random.normal(key_list[1], (D,), jnp.float32), 0.25, 1.75).astype(jnp.bfloat16)
    query_weight = bell_draw(key_list[2], (D, D), D ** -0.5, 0.125, ((1, 4),))
    key_weight = bell_draw(key_list[3], (D, D), D ** -0.5, 0.125, ((1, 4),))
    value_weight = bell_draw(key_list[4], (D, D), D ** -0.5, 0.125, ((1, 4),))
    head_gain = jnp.clip(1.0 + 0.15 * jax.random.normal(key_list[5], (D,), jnp.float32), 0.25, 1.75).astype(jnp.bfloat16)
    out_weight = bell_draw(key_list[6], (D, D), D ** -0.5, 0.125, ((0, 4),))
    moe_gain = jnp.clip(1.0 + 0.15 * jax.random.normal(key_list[7], (D,), jnp.float32), 0.25, 1.75).astype(jnp.bfloat16)
    route_ids_keys = jax.random.split(jax.random.fold_in(key_list[8], 1), LENGTH * BATCH // ROWS)
    route_ids_turns = jax.random.permutation(jax.random.fold_in(key_list[8], 3), LENGTH * BATCH // ROWS)
    route_ids = jax.vmap(lambda own, number: deal_out(jax.random.fold_in(key_list[8], 2), own, number, ROWS, EXPERTS, TOP, CAP, 2))(route_ids_keys, route_ids_turns).reshape((LENGTH, BATCH, TOP))
    route_weight = jnp.clip(0.05 + 0.25 * jax.random.uniform(key_list[9], (LENGTH, BATCH, TOP), jnp.float32) ** levels(key_list[9], (LENGTH, BATCH, TOP), ((0, 32),), -0.2, 0.2), 0.05, 0.3)
    expert_gate = bell_draw(key_list[10], (2 * EXPERTS, D, FF // 2), D ** -0.5, 0.125, ((0, 32),))
    expert_up = bell_draw(key_list[11], (2 * EXPERTS, D, FF // 2), D ** -0.5, 0.125, ((0, 32),))
    expert_down = bell_draw(key_list[12], (2 * EXPERTS, FF // 2, D), FF ** -0.5, 0.1875, ((0, 32),))
    return {"tokens": tokens, "attn_gain": attn_gain, "query_weight": query_weight, "key_weight": key_weight, "value_weight": value_weight, "head_gain": head_gain, "out_weight": out_weight, "moe_gain": moe_gain, "route_ids": route_ids, "route_weight": route_weight, "expert_gate": expert_gate, "expert_up": expert_up, "expert_down": expert_down}


norm_eps = 1e-05
head_eps = 1e-06

def root_scale(values, gain_values, epsilon):
    return values * lax.rsqrt(lax.optimization_barrier(jnp.mean(values * values, axis=-1, keepdims=True)) + epsilon) * gain_values.astype(jnp.float32)

def reference(tokens, attn_gain, query_weight, key_weight, value_weight, head_gain, out_weight, moe_gain, route_ids, route_weight, expert_gate, expert_up, expert_down):
    token_count = LENGTH * BATCH
    stream = tokens.astype(jnp.float32).reshape(token_count, D)
    normed = root_scale(stream, attn_gain, norm_eps).astype(jnp.bfloat16)
    block_shape = (N_SEQ, SPAN, BATCH, HEADS, HEAD_DIM)
    query_rows = jax.nn.silu(jnp.dot(normed, query_weight, preferred_element_type=jnp.float32)).astype(jnp.bfloat16).reshape(block_shape)
    key_rows = jax.nn.silu(jnp.dot(normed, key_weight, preferred_element_type=jnp.float32)).astype(jnp.bfloat16).reshape(block_shape)
    value_rows = jnp.dot(normed, value_weight, preferred_element_type=jnp.float32).astype(jnp.bfloat16).reshape(block_shape)

    def block_state(pair):
        return jnp.einsum('sbhd,sbhe->bhde', pair[0].astype(jnp.float32), pair[1].astype(jnp.float32))
    states = lax.map(block_state, (key_rows, value_rows))
    totals = jnp.cumsum(states, axis=0)
    carried = jnp.concatenate([jnp.zeros_like(states[:1]), totals[:-1]], axis=0)
    position = lax.broadcasted_iota(jnp.int32, (SPAN, SPAN), 0)
    key_position = lax.broadcasted_iota(jnp.int32, (SPAN, SPAN), 1)
    gain_heads = head_gain.reshape(HEADS, HEAD_DIM)

    def block_mix(group):
        query_block, key_block, value_block, carried_block = group
        scores = jnp.einsum('pbhd,sbhd->bhps', query_block.astype(jnp.float32), key_block.astype(jnp.float32))
        scores = jnp.where(position >= key_position, scores, 0.0).astype(jnp.bfloat16)
        local_mix = jnp.einsum('bhps,sbhd->pbhd', scores.astype(jnp.float32), value_block.astype(jnp.float32))
        carried_mix = jnp.einsum('pbhd,bhde->pbhe', query_block.astype(jnp.float32), carried_block, precision=lax.Precision.HIGHEST)
        return root_scale(local_mix + carried_mix, gain_heads, head_eps).astype(jnp.bfloat16)
    attended = lax.map(block_mix, (query_rows, key_rows, value_rows, carried)).reshape(token_count, D)
    group_width = D // N_HEAD
    projected = jnp.zeros((token_count, D), jnp.float32)
    for group_index in range(N_HEAD):
        lower_col = group_index * group_width
        group_term = jnp.dot(attended[:, lower_col:lower_col + group_width], out_weight[lower_col:lower_col + group_width], preferred_element_type=jnp.float32).astype(jnp.bfloat16)
        projected = projected + lax.optimization_barrier(group_term).astype(jnp.float32)
    residual_stream = stream + projected
    moe_input = root_scale(residual_stream, moe_gain, norm_eps).astype(jnp.bfloat16)
    route_count = ROWS * TOP
    expert_ids = route_ids.reshape(DEVICES, route_count)
    one_hot = (expert_ids[:, :, None] == jnp.arange(EXPERTS, dtype=jnp.int32)[None, None, :]).astype(jnp.int32)
    expert_slot = lax.optimization_barrier(jnp.sum(jnp.cumsum(one_hot, axis=1) * one_hot, axis=2)) - 1
    column = jnp.arange(DEVICES, dtype=jnp.int32)[:, None] * CAP + expert_slot
    token_index = (jnp.arange(DEVICES * route_count, dtype=jnp.int32) // TOP).reshape(DEVICES, route_count)
    row_table = jnp.full((EXPERTS, DEVICES * CAP), token_count, jnp.int32).at[expert_ids, column].set(token_index)
    weight_table = jnp.zeros((EXPERTS, DEVICES * CAP), jnp.float32).at[expert_ids, column].set(route_weight.reshape(DEVICES, route_count))
    padded_input = jnp.concatenate([moe_input, jnp.zeros((1, D), jnp.bfloat16)], axis=0)

    def expert_step(moe_total, expert_index):
        rows_index = row_table[expert_index]
        expert_rows = padded_input[rows_index]
        expert_sum = jnp.zeros((DEVICES * CAP, D), jnp.float32)
        for half_index in range(2):
            half_slot = 2 * expert_index + half_index
            gate_rows = jnp.dot(expert_rows, expert_gate[half_slot], preferred_element_type=jnp.float32)
            up_rows = jnp.dot(expert_rows, expert_up[half_slot], preferred_element_type=jnp.float32)
            activated = (jax.nn.silu(gate_rows) * up_rows).astype(jnp.bfloat16)
            half_output = jnp.dot(activated, expert_down[half_slot], preferred_element_type=jnp.float32).astype(jnp.bfloat16)
            expert_sum = expert_sum + lax.optimization_barrier(half_output).astype(jnp.float32)
        rounded_sum = lax.optimization_barrier(expert_sum.astype(jnp.bfloat16)).astype(jnp.float32)
        moe_total = moe_total.at[rows_index].add(rounded_sum * weight_table[expert_index][:, None])
        return (moe_total, None)
    moe_total, unused_out = lax.scan(expert_step, jnp.zeros((token_count + 1, D), jnp.float32), jnp.arange(EXPERTS, dtype=jnp.int32))
    moe_output = moe_total[:token_count]
    return (residual_stream + moe_output).astype(jnp.bfloat16).reshape(LENGTH, BATCH, D)
```

```python
import jax
import jax.numpy as jnp
from jax import lax
from jax.sharding import PartitionSpec as P

HEAD_DIM = 128
EXPERTS = 64
TOP = 8


norm_eps = 1e-05
head_eps = 1e-06


def root_scale(values, gain_values, epsilon):
    return (
        values
        * lax.rsqrt(jnp.mean(values * values, axis=-1, keepdims=True) + epsilon)
        * gain_values.astype(jnp.float32)
    )


def body(
    tokens,
    attn_gain,
    query_weight,
    key_weight,
    value_weight,
    head_gain,
    out_weight,
    moe_gain,
    route_ids,
    route_weight,
    expert_gate,
    expert_up,
    expert_down,
):
    head_count = lax.axis_size("head")
    seq_count = lax.axis_size("seq")
    gathered = lax.all_gather(tokens, "head", axis=2, tiled=True)
    block_len, batch_size, model_width = gathered.shape
    stream = gathered.astype(jnp.float32)
    normed = root_scale(stream, attn_gain, norm_eps).astype(jnp.bfloat16)
    heads_local = query_weight.shape[1] // HEAD_DIM
    head_shape = (block_len, batch_size, heads_local, HEAD_DIM)

    def project(weight):
        return jnp.dot(normed, weight, preferred_element_type=jnp.float32)

    query_rows = jax.nn.silu(project(query_weight)).astype(jnp.bfloat16).reshape(head_shape)
    key_rows = jax.nn.silu(project(key_weight)).astype(jnp.bfloat16).reshape(head_shape)
    value_rows = project(value_weight).astype(jnp.bfloat16).reshape(head_shape)
    position = lax.broadcasted_iota(jnp.int32, (block_len, block_len), 0)
    key_position = lax.broadcasted_iota(jnp.int32, (block_len, block_len), 1)
    scores = jnp.einsum("pbhd,sbhd->bhps", query_rows, key_rows, preferred_element_type=jnp.float32)
    scores = jnp.where(position >= key_position, scores, 0.0).astype(jnp.bfloat16)
    local_mix = jnp.einsum(
        "bhps,sbhd->pbhd", scores, value_rows, preferred_element_type=jnp.float32
    )
    local_state = jnp.einsum(
        "sbhd,sbhe->bhde", key_rows, value_rows, preferred_element_type=jnp.float32
    )

    all_states = lax.all_gather(local_state.astype(jnp.bfloat16), "seq", axis=0, tiled=False)
    earlier = jnp.arange(seq_count, dtype=jnp.int32) < lax.axis_index("seq")
    carried = jnp.sum(
        jnp.where(earlier[:, None, None, None, None], all_states.astype(jnp.float32), 0.0), axis=0
    )
    carried_mix = jnp.einsum(
        "pbhd,bhde->pbhe", query_rows.astype(jnp.float32), carried, precision=lax.Precision.HIGHEST
    )
    mixed_heads = local_mix + carried_mix
    attended = root_scale(mixed_heads, head_gain.reshape(heads_local, HEAD_DIM), head_eps).astype(
        jnp.bfloat16
    )
    attended = attended.reshape(block_len, batch_size, heads_local * HEAD_DIM)
    own_rows = block_len // head_count
    row_term = jnp.dot(attended, out_weight, preferred_element_type=jnp.float32).astype(
        jnp.bfloat16
    )
    projected = lax.psum_scatter(
        lax.optimization_barrier(row_term).astype(jnp.float32).astype(jnp.bfloat16),
        "head",
        scatter_dimension=0,
        tiled=True,
    ).astype(jnp.float32)
    own_stream = lax.dynamic_slice_in_dim(stream, lax.axis_index("head") * own_rows, own_rows, 0)
    total_rows = own_rows * batch_size
    residual_stream = (own_stream + projected).reshape(total_rows, model_width)
    moe_input = root_scale(residual_stream, moe_gain, norm_eps).astype(jnp.bfloat16)
    capacity = max(2, 3 * total_rows * TOP // (2 * EXPERTS))
    device_count = seq_count * head_count
    both = ("seq", "head")
    halves_local = expert_gate.shape[0]
    device_rank = lax.axis_index("seq") * head_count + lax.axis_index("head")
    routes = jnp.concatenate(
        [
            route_ids.reshape(total_rows, TOP).astype(jnp.float32),
            route_weight.reshape(total_rows, TOP),
        ],
        axis=1,
    )
    routes = lax.all_gather(routes, both, axis=0, tiled=False)
    ids = routes[:, :, :TOP].astype(jnp.int32)
    weights = routes[:, :, TOP:]
    per = max(1, halves_local // 2)
    share = halves_local // per
    own_experts = device_rank * halves_local // 2 + jnp.arange(per, dtype=jnp.int32)
    named = ids[:, None, :, :] == own_experts[None, :, None, None]
    match = jnp.any(named, axis=3)
    gate_weight = jnp.sum(jnp.where(named, weights[:, None], 0.0), axis=3)
    row_index = lax.broadcasted_iota(jnp.int32, (total_rows, total_rows), 0)
    col_index = lax.broadcasted_iota(jnp.int32, (total_rows, total_rows), 1)
    before = (row_index < col_index).astype(jnp.bfloat16)
    slot = jnp.einsum(
        "blt,tu->blu", match.astype(jnp.bfloat16), before, preferred_element_type=jnp.float32
    ).astype(jnp.int32)
    slots = jnp.arange(capacity, dtype=jnp.int32)
    placed = match[:, :, None, :] & (slot[:, :, None, :] == slots[None, None, :, None])
    pick = placed.astype(jnp.bfloat16).reshape(device_count, per * capacity, total_rows)
    blend = jnp.where(placed, gate_weight[:, :, None, :], 0.0).astype(jnp.bfloat16)
    blend = blend.reshape(device_count, per * capacity, total_rows)
    rows = lax.all_gather(moe_input, both, axis=0, tiled=False)
    picked = jnp.einsum("bst,btd->bsd", pick, rows, preferred_element_type=jnp.float32)
    picked = picked.astype(jnp.bfloat16).reshape(device_count, per, capacity, model_width)
    sums = []
    for local in range(per):
        expert_rows = picked[:, local].reshape(device_count * capacity, model_width)
        total = None
        for half in range(share):
            index = local * share + half
            gate_rows = jnp.dot(
                expert_rows, expert_gate[index], preferred_element_type=jnp.float32
            )
            up_rows = jnp.dot(expert_rows, expert_up[index], preferred_element_type=jnp.float32)
            activated = (jax.nn.silu(gate_rows) * up_rows).astype(jnp.bfloat16)
            part = jnp.dot(activated, expert_down[index], preferred_element_type=jnp.float32)
            total = part if total is None else total + part
        sums.append(
            total.astype(jnp.bfloat16).reshape(device_count, 1, capacity, model_width)
        )
    expert_sum = jnp.concatenate(sums, axis=1).reshape(device_count, per * capacity, model_width)
    partial = jnp.einsum("bst,bsd->btd", blend, expert_sum, preferred_element_type=jnp.float32)
    moe_output = lax.psum_scatter(
        partial.astype(jnp.bfloat16), both, scatter_dimension=0, tiled=False
    ).astype(jnp.float32)
    return (
        (residual_stream + moe_output)
        .astype(jnp.bfloat16)
        .reshape(own_rows, batch_size, model_width)
    )


def solution(mesh):
    in_specs = (
        P("seq", None, "head"),
        P(),
        P(None, "head"),
        P(None, "head"),
        P(None, "head"),
        P("head"),
        P("head", None),
        P(),
        P(("seq", "head"), None, None),
        P(("seq", "head"), None, None),
        P(("seq", "head"), None, None),
        P(("seq", "head"), None, None),
        P(("seq", "head"), None, None),
    )
    out_specs = P(("seq", "head"), None, None)
    return jax.shard_map(body, mesh=mesh, in_specs=in_specs, out_specs=out_specs, check_vma=False)
```

```python
import jax
import jax.numpy as jnp
from jax import lax
from jax.sharding import PartitionSpec as P

HEAD_DIM = 128
EXPERTS = 64
TOP = 8


norm_eps = 1e-05
head_eps = 1e-06


def root_scale(values, gain_values, epsilon):
    return (
        values
        * lax.rsqrt(jnp.mean(values * values, axis=-1, keepdims=True) + epsilon)
        * gain_values.astype(jnp.float32)
    )


def body(
    tokens,
    attn_gain,
    query_weight,
    key_weight,
    value_weight,
    head_gain,
    out_weight,
    moe_gain,
    route_ids,
    route_weight,
    expert_gate,
    expert_up,
    expert_down,
):
    head_count = lax.axis_size("head")
    seq_count = lax.axis_size("seq")
    gathered = lax.all_gather(tokens, "head", axis=2, tiled=True)
    block_len, batch_size, model_width = gathered.shape
    both = ("seq", "head")
    own_routes = jnp.concatenate(
        [route_ids.reshape(-1, TOP).astype(jnp.float32), route_weight.reshape(-1, TOP)], axis=1
    )
    routes = lax.all_gather(own_routes, both, axis=0, tiled=False)
    gathered, routes = lax.optimization_barrier((gathered, routes))
    stream = gathered.astype(jnp.float32)
    normed = root_scale(stream, attn_gain, norm_eps).astype(jnp.bfloat16)
    heads_local = query_weight.shape[1] // HEAD_DIM
    head_shape = (block_len, batch_size, heads_local, HEAD_DIM)

    def project(weight):
        return jnp.dot(normed, weight, preferred_element_type=jnp.float32)

    query_rows = jax.nn.silu(project(query_weight)).astype(jnp.bfloat16).reshape(head_shape)
    key_rows = jax.nn.silu(project(key_weight)).astype(jnp.bfloat16).reshape(head_shape)
    value_rows = project(value_weight).astype(jnp.bfloat16).reshape(head_shape)
    position = lax.broadcasted_iota(jnp.int32, (block_len, block_len), 0)
    key_position = lax.broadcasted_iota(jnp.int32, (block_len, block_len), 1)
    scores = jnp.einsum("pbhd,sbhd->bhps", query_rows, key_rows, preferred_element_type=jnp.float32)
    scores = jnp.where(position >= key_position, scores, 0.0).astype(jnp.bfloat16)
    local_mix = jnp.einsum(
        "bhps,sbhd->pbhd", scores, value_rows, preferred_element_type=jnp.float32
    )
    local_state = jnp.einsum(
        "sbhd,sbhe->bhde", key_rows, value_rows, preferred_element_type=jnp.float32
    )

    shares = local_state.astype(jnp.bfloat16).reshape(seq_count, -1, HEAD_DIM)
    shares = lax.all_to_all(shares, "seq", split_axis=0, concat_axis=0, tiled=True)
    running = jnp.zeros(shares.shape[1:], jnp.float32)
    prefixes = []
    for block in range(seq_count):
        prefixes.append(running.astype(jnp.bfloat16))
        running = running + shares[block].astype(jnp.float32)
    carried = lax.all_to_all(jnp.stack(prefixes), "seq", split_axis=0, concat_axis=0, tiled=True)
    carried = carried.reshape(local_state.shape).astype(jnp.float32)
    carried_mix = jnp.einsum(
        "pbhd,bhde->pbhe", query_rows.astype(jnp.float32), carried, precision=lax.Precision.HIGHEST
    )
    mixed_heads = local_mix + carried_mix
    attended = root_scale(mixed_heads, head_gain.reshape(heads_local, HEAD_DIM), head_eps).astype(
        jnp.bfloat16
    )
    attended = attended.reshape(block_len, batch_size, heads_local * HEAD_DIM)
    own_rows = block_len // head_count
    row_term = jnp.dot(attended, out_weight, preferred_element_type=jnp.float32).astype(
        jnp.bfloat16
    )
    projected = lax.psum_scatter(
        lax.optimization_barrier(row_term).astype(jnp.float32).astype(jnp.bfloat16),
        "head",
        scatter_dimension=0,
        tiled=True,
    ).astype(jnp.float32)
    own_stream = lax.dynamic_slice_in_dim(stream, lax.axis_index("head") * own_rows, own_rows, 0)
    total_rows = own_rows * batch_size
    residual_stream = (own_stream + projected).reshape(total_rows, model_width)
    moe_input = root_scale(residual_stream, moe_gain, norm_eps).astype(jnp.bfloat16)
    capacity = max(2, 3 * total_rows * TOP // (2 * EXPERTS))
    device_count = seq_count * head_count
    halves_local = expert_gate.shape[0]
    device_rank = lax.axis_index("seq") * head_count + lax.axis_index("head")
    ids = routes[:, :, :TOP].astype(jnp.int32)
    weights = routes[:, :, TOP:]
    per = max(1, halves_local // 2)
    share = halves_local // per
    own_experts = device_rank * halves_local // 2 + jnp.arange(per, dtype=jnp.int32)
    row_index = lax.broadcasted_iota(jnp.int32, (total_rows, total_rows), 0)
    col_index = lax.broadcasted_iota(jnp.int32, (total_rows, total_rows), 1)
    before = (row_index < col_index).astype(jnp.bfloat16)
    slots = jnp.arange(capacity, dtype=jnp.int32)

    def tables(ids, weights, experts):
        named = ids[:, None, :, :] == experts[:, :, None, None]
        match = jnp.any(named, axis=3)
        gate_weight = jnp.sum(jnp.where(named, weights[:, None], 0.0), axis=3)
        slot = jnp.einsum(
            "blt,tu->blu", match.astype(jnp.bfloat16), before, preferred_element_type=jnp.float32
        ).astype(jnp.int32)
        placed = match[:, :, None, :] & (slot[:, :, None, :] == slots[None, None, :, None])
        blend = jnp.where(placed, gate_weight[:, :, None, :], 0.0).astype(jnp.bfloat16)
        shape = (device_count, per * capacity, total_rows)
        return placed.astype(jnp.bfloat16).reshape(shape), blend.reshape(shape)

    pick, blend = tables(ids, weights, own_experts[None])
    all_experts = (
        jnp.arange(device_count, dtype=jnp.int32)[:, None] * halves_local // 2
        + jnp.arange(per, dtype=jnp.int32)[None]
    )
    own_pick, own_blend = tables(
        own_routes[None, :, :TOP].astype(jnp.int32), own_routes[None, :, TOP:], all_experts
    )
    cut_in = model_width * 5 // 8
    cut_out = model_width // 2
    sending = jnp.einsum(
        "bst,td->bsd", own_pick, moe_input[:, cut_in:], preferred_element_type=jnp.float32
    ).astype(jnp.bfloat16)
    rows = lax.all_gather(moe_input[:, :cut_in], both, axis=0, tiled=False)
    received = lax.all_to_all(sending, both, split_axis=0, concat_axis=0, tiled=True)
    picked = jnp.einsum(
        "bst,btd->bsd", pick, rows, preferred_element_type=jnp.float32
    ).astype(jnp.bfloat16)
    picked = jnp.concatenate([picked, received], axis=2)
    picked = picked.reshape(device_count, per, capacity, model_width)
    hidden = []
    for local in range(per):
        expert_rows = picked[:, local].reshape(device_count * capacity, model_width)
        for half in range(share):
            index = local * share + half
            gate_rows = jnp.dot(
                expert_rows, expert_gate[index], preferred_element_type=jnp.float32
            )
            up_rows = jnp.dot(expert_rows, expert_up[index], preferred_element_type=jnp.float32)
            hidden.append((jax.nn.silu(gate_rows) * up_rows).astype(jnp.bfloat16))

    def summed(hidden, low, high):
        sums = []
        for local in range(per):
            total = 0.0
            for index in range(local * share, (local + 1) * share):
                total = total + jnp.dot(
                    hidden[index],
                    expert_down[index, :, low:high],
                    preferred_element_type=jnp.float32,
                )
            sums.append(
                total.astype(jnp.bfloat16).reshape(device_count, 1, capacity, high - low)
            )
        return jnp.concatenate(sums, axis=1).reshape(device_count, per * capacity, high - low)

    partial = jnp.einsum(
        "bst,bsd->btd",
        blend,
        summed(hidden, 0, cut_out),
        preferred_element_type=jnp.float32,
    ).astype(jnp.bfloat16)
    partial, hidden = lax.optimization_barrier((partial, hidden))
    lower = lax.psum_scatter(partial, both, scatter_dimension=0, tiled=False)
    returned = lax.all_to_all(
        summed(hidden, cut_out, model_width), both, split_axis=0, concat_axis=0, tiled=True
    )
    upper = jnp.einsum(
        "kt,kd->td",
        own_blend.reshape(-1, total_rows),
        returned.reshape(-1, model_width - cut_out),
        preferred_element_type=jnp.float32,
    )
    moe_output = jnp.concatenate([lower.astype(jnp.float32), upper], axis=1)
    return (
        (residual_stream + moe_output)
        .astype(jnp.bfloat16)
        .reshape(own_rows, batch_size, model_width)
    )


def solution(mesh):
    in_specs = (
        P("seq", None, "head"),
        P(),
        P(None, "head"),
        P(None, "head"),
        P(None, "head"),
        P("head"),
        P("head", None),
        P(),
        P(("seq", "head"), None, None),
        P(("seq", "head"), None, None),
        P(("seq", "head"), None, None),
        P(("seq", "head"), None, None),
        P(("seq", "head"), None, None),
    )
    out_specs = P(("seq", "head"), None, None)
    return jax.shard_map(body, mesh=mesh, in_specs=in_specs, out_specs=out_specs, check_vma=False)
```
